32 devices in a mesh: tm: 16 (over z, x, core), dp: 2 (over y).
Axes of the slice: x: 2, y: 2, z: 4, core: 2. Of those that a mesh axis runs over, the one named last changes fastest.
Arguments:
- queries: bfloat16 [2, 4096, 1024], P('dp', 'tm'), may hold values from -40 to 40
- keys: bfloat16 [2, 4096, 1024], P('dp', 'tm'), may hold values from -40 to 40
- values: bfloat16 [2, 4096, 1024], P('dp', 'tm'), may hold values from -6 to 6
- out_grad: bfloat16 [2, 4096, 1024], P('dp', 'tm'), may hold values from -6 to 6
- temper: float32 [8], replicated, may hold values from 0.5 to 2
Outputs:
- attended: bfloat16 [2, 4096, 1024], P('dp', 'tm')
- query_grad: bfloat16 [2, 4096, 1024], P('dp', 'tm')
- key_grad: bfloat16 [2, 4096, 1024], P('dp', 'tm')
- value_grad: bfloat16 [2, 4096, 1024], P('dp', 'tm')
- temper_grad: float32 [8], replicated
The draws below stay inside these ranges and needn't reach their ends.
All inputs are finite; a program needn't handle non-finite values.
Results may differ from the reference program's by a relative error of at most 0.0083.
Values may be sent and summed in bfloat16 or wider, within the bound.
No kernel may reach another device: no remote copies, remote signals or barrier semaphores. Data moves between devices by JAX's collectives and lax.ppermute only.
A program may use at most 64 MiB of HBM per device.

```python
import math
import jax
import jax.numpy as jnp
from jax import lax

HEADS = 8
HEAD_DIM = 128
GROUP = 256
SEQS = 2
SEQLEN = 4096


def pair_draw(key):
    shape = (SEQS, SEQLEN, HEADS * HEAD_DIM)
    first, second = jax.random.split(key)
    query_base = jnp.clip(jax.random.normal(first, shape, jnp.float32), -4.0, 4.0)
    key_base = jnp.clip(jax.random.normal(second, shape, jnp.float32), -4.0, 4.0)
    return (query_base, key_base)


def draw_queries(key, part):
    return pair_draw(key)[0].astype(jnp.bfloat16)


def draw_keys(key, part):
    return pair_draw(key)[1].astype(jnp.bfloat16)


def block_levels(key, extent, shards, least, high):
    def one(axis_at, blocks):
        heights = jax.random.uniform(jax.random.fold_in(jax.random.fold_in(key, 6), axis_at), (blocks,), jnp.float32, least / len(shards), high / len(shards))
        return jnp.repeat(jnp.exp(heights), extent[axis_at] // blocks).reshape((-1,) + (1,) * (len(extent) - axis_at - 1))

    gain = one(*shards[0])
    for cut in shards[1:]:
        gain = gain * one(*cut)
    return gain


def normal_values(own_key, shape, spread, reach, shards=(), kind=jnp.bfloat16):
    factor_of = block_levels(own_key, shape, shards, -0.22, 0.18) if shards else 1.0
    drawn = jax.random.normal(own_key, shape, jnp.float32) * spread * factor_of
    return jnp.minimum(jnp.maximum(drawn, -reach), reach).astype(kind)


def setup_inputs(seed: int = 0) -> dict:
    key_of = jax.random.split(jax.random.key(seed), 6)
    return {
        "queries": draw_queries(jax.random.fold_in(key_of[5], 71), 0),
        "keys": draw_keys(jax.random.fold_in(key_of[5], 71), 0),
        "values": normal_values(key_of[2], (SEQS, SEQLEN, HEADS * HEAD_DIM), 1.0, 6.0, ((0, 2), (1, 16))),
        "out_grad": normal_values(key_of[3], (SEQS, SEQLEN, HEADS * HEAD_DIM), 1.0, 6.0, ((0, 2), (1, 16))),
        "temper": jnp.clip(jnp.exp(jax.random.uniform(key_of[4], (HEADS,), jnp.float32, math.log(0.5), math.log(2.0))), 0.5, 2.0),
    }


def split_heads(array):
    return array.reshape(array.shape[0], array.shape[1], HEADS, HEAD_DIM).astype(jnp.float32)

def attend_block(query_rows, key_rows, value_rows, grad_rows, temper, valid):
    batch = query_rows.shape[0]
    length = query_rows.shape[1]
    span = key_rows.shape[1]
    query_heads = split_heads(query_rows)
    key_heads = split_heads(key_rows)
    value_heads = split_heads(value_rows)
    grad_heads = split_heads(grad_rows)
    root = math.sqrt(HEAD_DIM)
    raw_scores = jnp.einsum('sihd,sjhd->shij', query_heads, key_heads) / root
    scores = raw_scores * temper[None, :, None, None]
    scores = jnp.where(valid[None, None, None, :], scores, -1e+30)
    highest = lax.optimization_barrier(jnp.max(scores, axis=-1, keepdims=True))
    expo = jnp.exp(scores - highest)
    probs = expo / lax.optimization_barrier(jnp.sum(expo, axis=-1, keepdims=True))
    probs_low = lax.optimization_barrier(probs.astype(jnp.bfloat16)).astype(jnp.float32)
    attended = jnp.einsum('shij,sjhd->sihd', probs_low, value_heads)
    attended = attended.reshape(batch, length, -1).astype(jnp.bfloat16)
    prob_grad = jnp.einsum('sihd,sjhd->shij', grad_heads, value_heads)
    delta = lax.optimization_barrier(jnp.sum(probs * prob_grad, axis=-1, keepdims=True))
    score_grad = probs * (prob_grad - delta)
    score_low = lax.optimization_barrier(score_grad.astype(jnp.bfloat16)).astype(jnp.float32)
    factor = (temper / root)[None, None, :, None]
    query_grad = jnp.einsum('shij,sjhd->sihd', score_low, key_heads) * factor
    query_grad = query_grad.reshape(batch, length, -1).astype(jnp.bfloat16)
    key_part = (jnp.einsum('shij,sihd->sjhd', score_low, query_heads) * factor).reshape(batch, span, -1)
    value_part = jnp.einsum('shij,sihd->sjhd', probs_low, grad_heads).reshape(batch, span, -1)
    key_part = lax.optimization_barrier(key_part.astype(jnp.bfloat16)).astype(jnp.float32)
    value_part = lax.optimization_barrier(value_part.astype(jnp.bfloat16)).astype(jnp.float32)
    temper_part = lax.optimization_barrier(jnp.sum(score_grad * raw_scores, axis=(0, 2, 3)))
    return (attended, query_grad, key_part, value_part, temper_part)

def reference(queries, keys, values, out_grad, temper):
    front = 2 * GROUP
    width = HEADS * HEAD_DIM
    padding = ((0, 0), (front, 0), (0, 0))
    key_pad = jnp.pad(keys, padding)
    value_pad = jnp.pad(values, padding)
    blocks = SEQLEN // GROUP
    start_state = (jnp.zeros((SEQS, SEQLEN + front, width), jnp.float32), jnp.zeros((SEQS, SEQLEN + front, width), jnp.float32), jnp.zeros((HEADS,), jnp.float32))

    def step(carry, block_index):
        key_total, value_total, temper_total = carry
        start = (block_index * GROUP).astype(jnp.int32)
        query_rows = lax.dynamic_slice_in_dim(queries, start, GROUP, 1)
        grad_rows = lax.dynamic_slice_in_dim(out_grad, start, GROUP, 1)
        key_rows = lax.dynamic_slice_in_dim(key_pad, start, 3 * GROUP, 1)
        value_rows = lax.dynamic_slice_in_dim(value_pad, start, 3 * GROUP, 1)
        valid = block_index + jnp.arange(3 * GROUP, dtype=jnp.int32) // GROUP - 2 >= 0
        attended, query_grad, key_part, value_part, temper_part = attend_block(query_rows, key_rows, value_rows, grad_rows, temper, valid)
        key_total = lax.dynamic_update_slice_in_dim(key_total, lax.dynamic_slice_in_dim(key_total, start, 3 * GROUP, 1) + key_part, start, 1)
        value_total = lax.dynamic_update_slice_in_dim(value_total, lax.dynamic_slice_in_dim(value_total, start, 3 * GROUP, 1) + value_part, start, 1)
        return ((key_total, value_total, temper_total + temper_part), (attended, query_grad))
    final, stacked = lax.scan(step, start_state, jnp.arange(blocks, dtype=jnp.int32))
    key_total, value_total, temper_grad = final
    attended = jnp.transpose(stacked[0], (1, 0, 2, 3)).reshape(SEQS, SEQLEN, width)
    query_grad = jnp.transpose(stacked[1], (1, 0, 2, 3)).reshape(SEQS, SEQLEN, width)
    key_grad = key_total[:, front:].astype(jnp.bfloat16)
    value_grad = value_total[:, front:].astype(jnp.bfloat16)
    return (attended, query_grad, key_grad, value_grad, temper_grad)
```

```python
import math

import jax
import jax.numpy as jnp
from jax import lax
from jax.experimental import pallas as pl
from jax.experimental.pallas import tpu as pltpu
from jax.sharding import PartitionSpec as P

HEADS = 8
HEAD_DIM = 128
LOG2E = math.log2(math.e)
CHUNKS = (4, 4)
VMEM_LIMIT = 32 * 1024 * 1024


def shift(value, axis, by, parity=None):
    peers = lax.axis_size(axis)
    pairs = [
        (i, i + by)
        for i in range(peers)
        if 0 <= i + by < peers and (parity is None or i % 2 == parity)
    ]
    return lax.ppermute(value, axis, pairs)


def swap(value, axis, mask=1):
    peers = lax.axis_size(axis)
    return lax.ppermute(value, axis, [(i, i ^ mask) for i in range(peers)])


def sum_everywhere(value, axes):
    for axis in axes:
        peers = lax.axis_size(axis)
        if peers & (peers - 1):
            parts = [value]
            for by in range(1, peers):
                pairs = [(i, (i + by) % peers) for i in range(peers)]
                parts.append(lax.ppermute(value, axis, pairs))
            at = lax.axis_index(axis)
            stacked = jnp.roll(jnp.stack(parts[:1] + parts[:0:-1]), at, axis=0)
            value = jnp.sum(stacked, axis=0)
            continue
        mask = 1
        while mask < peers:
            value = value + swap(value, axis, mask)
            mask *= 2
    return value


def pack_kernel(k_ref, v_ref, out_ref):
    out_ref[0] = k_ref[0]
    out_ref[1] = v_ref[0]


def pack(keys, values, first, heads):
    length = keys.shape[1]
    spec = pl.BlockSpec((1, length, HEAD_DIM), lambda i: (0, 0, first + i))
    return pl.pallas_call(
        pack_kernel,
        grid=(heads,),
        in_specs=[spec, spec],
        out_specs=pl.BlockSpec((2, length, HEAD_DIM), lambda i: (0, 0, i)),
        out_shape=jax.ShapeDtypeStruct((2, length, heads * HEAD_DIM), keys.dtype),
        compiler_params=pltpu.CompilerParams(vmem_limit_bytes=VMEM_LIMIT),
        cost_estimate=pl.CostEstimate(
            flops=0, bytes_accessed=8 * length * heads * HEAD_DIM, transcendentals=0
        ),
    )(keys, values)


def dot_nt(a, b):
    return lax.dot_general(a, b, (((1,), (1,)), ((), ())), preferred_element_type=jnp.float32)


def dot_tn(a, b):
    return lax.dot_general(a, b, (((0,), (0,)), ((), ())), preferred_element_type=jnp.float32)


def dot_nn(a, b):
    return jnp.dot(a, b, preferred_element_type=jnp.float32)


def attend_kernel(
    first,
    pos_ref,
    temper_ref,
    q_ref,
    g_ref,
    k_ref,
    v_ref,
    far_ref,
    near_a_ref,
    near_b_ref,
    *refs,
):
    o_ref, dq_ref, own_ref, near_ref, out_far_ref, t_ref = refs[-6:]
    pos = pos_ref[0]
    temper = temper_ref[first + pl.program_id(0)]
    root = math.sqrt(HEAD_DIM)
    factor = temper / root
    scale = factor * LOG2E
    q = q_ref[0]
    g = g_ref[0]
    keys = [far_ref[0], near_a_ref[0] + near_b_ref[0], k_ref[0]]
    values = [far_ref[1], near_a_ref[1] + near_b_ref[1], v_ref[0]]
    lows = [
        jnp.where(pos >= 2, 0.0, -1e30).astype(jnp.float32),
        jnp.where(pos >= 1, 0.0, -1e30).astype(jnp.float32),
        None,
    ]
    scores = []
    for key, low in zip(keys, lows):
        s = dot_nt(key, q) * scale
        scores.append(s if low is None else s + low)
    highest = jnp.max(scores[0], axis=0, keepdims=True)
    for s in scores[1:]:
        highest = jnp.maximum(highest, jnp.max(s, axis=0, keepdims=True))
    expo = [jnp.exp2(s - highest) for s in scores]
    total = sum(jnp.sum(e, axis=0, keepdims=True) for e in expo)
    inverse = 1.0 / total
    probs = [e * inverse for e in expo]
    lows_p = [p.astype(jnp.bfloat16) for p in probs]
    grads = [dot_nt(value, g) for value in values]
    delta = sum(jnp.sum(p * d, axis=0, keepdims=True) for p, d in zip(probs, grads))
    score_grads = [p * (d - delta) for p, d in zip(probs, grads)]
    lows_s = [s.astype(jnp.bfloat16) for s in score_grads]
    row = sum(
        jnp.sum(d * s, axis=0, keepdims=True) for d, s in zip(score_grads, scores)
    )
    t_ref[0] = jnp.broadcast_to(
        jnp.sum(row, axis=1, keepdims=True) / (temper * LOG2E), (1, HEAD_DIM)
    )
    attended = sum(dot_tn(value, p) for value, p in zip(values, lows_p))
    query_grad = sum(dot_tn(key, s) for key, s in zip(keys, lows_s))
    o_ref[0] = attended.T.astype(o_ref.dtype)
    dq_ref[0] = (query_grad * factor).T.astype(dq_ref.dtype)
    for ref, p, s in zip((out_far_ref, near_ref, own_ref), lows_p, lows_s):
        ref[0] = (dot_nn(s, q) * factor).astype(ref.dtype)
        ref[1] = dot_nn(p, g).astype(ref.dtype)


def attend(first, heads, pos, temper, q, g, k, v, far, near_a, near_b, before):
    length = q.shape[1]
    wide = pl.BlockSpec((1, length, HEAD_DIM), lambda i: (0, 0, first + i))
    pair = pl.BlockSpec((2, length, HEAD_DIM), lambda i: (0, 0, i))
    smem = pl.BlockSpec(memory_space=pltpu.SMEM)
    in_specs = [smem, smem, wide, wide, wide, wide, pair, pair, pair]
    args = [pos, temper, q, g, k, v, far, near_a, near_b]
    aliases = {}
    if before is not None:
        aliases = {len(args): 0, len(args) + 1: 1}
        in_specs += [pl.BlockSpec(memory_space=pl.ANY)] * 2
        args += list(before)
    full = jax.ShapeDtypeStruct(q.shape, jnp.bfloat16)
    part = jax.ShapeDtypeStruct((2, length, heads * HEAD_DIM), jnp.bfloat16)
    return pl.pallas_call(
        lambda *refs: attend_kernel(first, *refs),
        grid=(heads,),
        in_specs=in_specs,
        out_specs=[wide, wide, pair, pair, pair, pl.BlockSpec((1, 1, HEAD_DIM), lambda i: (i, 0, 0))],
        out_shape=[full, full, part, part, part, jax.ShapeDtypeStruct((heads, 1, HEAD_DIM), jnp.float32)],
        input_output_aliases=aliases,
        compiler_params=pltpu.CompilerParams(vmem_limit_bytes=VMEM_LIMIT),
        cost_estimate=pl.CostEstimate(
            flops=heads * 18 * 2 * length * length * HEAD_DIM * 3,
            bytes_accessed=heads * 18 * 2 * length * HEAD_DIM,
            transcendentals=heads * 3 * length * length,
        ),
    )(*args)


def finish_kernel(odd_ref, own_ref, near_ref, back_ref, *refs):
    dk_ref, dv_ref = refs[-2:]
    even = odd_ref[0] == 0
    for at, ref in enumerate((dk_ref, dv_ref)):
        near = near_ref[at].astype(jnp.float32)
        near = jnp.where(even, near, jnp.zeros_like(near))
        total = own_ref[at].astype(jnp.float32) + near + back_ref[at].astype(jnp.float32)
        ref[0] = total.astype(ref.dtype)


def finish(first, heads, odd, own, near, back, shape, before):
    length = shape[1]
    wide = pl.BlockSpec((1, length, HEAD_DIM), lambda i: (0, 0, first + i))
    pair = pl.BlockSpec((2, length, HEAD_DIM), lambda i: (0, 0, i))
    in_specs = [pl.BlockSpec(memory_space=pltpu.SMEM), pair, pair, pair]
    args = [odd, own, near, back]
    aliases = {}
    if before is not None:
        aliases = {len(args): 0, len(args) + 1: 1}
        in_specs += [pl.BlockSpec(memory_space=pl.ANY)] * 2
        args += list(before)
    full = jax.ShapeDtypeStruct(shape, jnp.bfloat16)
    return pl.pallas_call(
        finish_kernel,
        grid=(heads,),
        in_specs=in_specs,
        out_specs=[wide, wide],
        out_shape=[full, full],
        input_output_aliases=aliases,
        compiler_params=pltpu.CompilerParams(vmem_limit_bytes=VMEM_LIMIT),
        cost_estimate=pl.CostEstimate(
            flops=0, bytes_accessed=heads * 8 * 2 * length * HEAD_DIM, transcendentals=0
        ),
    )(*args)


def on_device(queries, keys, values, out_grad, temper):
    pos = lax.axis_index("tm").astype(jnp.int32)
    odd = pos % 2
    pos_in, odd_in = pos[None], odd[None]
    starts = [sum(CHUNKS[:i]) for i in range(len(CHUNKS))]
    packed = [pack(keys, values, first, heads) for first, heads in zip(starts, CHUNKS)]
    fars = [shift(both, "tm", 2) for both in packed]
    nears = [shift(both, "tm", 1, parity=0) for both in packed]
    result, grads = None, None
    temper_parts = []
    pending = []
    for at, (first, heads) in enumerate(zip(starts, CHUNKS)):
        passed = shift(fars[at], "tm", -1, parity=1)
        outs = attend(
            first, heads, pos_in, temper, queries, out_grad, keys, values,
            fars[at], nears[at], passed, result,
        )
        result = (outs[0], outs[1])
        own, near, far, temper_part = outs[2:]
        temper_parts.append(temper_part)
        swapped = swap(near, "tm")
        send = jnp.where(
            odd == 1, (far.astype(jnp.float32) + swapped.astype(jnp.float32)).astype(jnp.bfloat16), far
        )
        pending.append((own, swapped, shift(send, "tm", -2)))
    temper_part = jnp.concatenate(temper_parts, axis=0)[:, 0, :]
    temper_grad = sum_everywhere(temper_part, ("tm", "dp"))[:, 0]
    for (first, heads), (own, swapped, back) in zip(zip(starts, CHUNKS), pending):
        grads = finish(first, heads, odd_in, own, swapped, back, keys.shape, grads)
    return (result[0], result[1], grads[0], grads[1], temper_grad)


def solution(mesh):
    rows = P("dp", "tm", None)
    return jax.shard_map(
        on_device,
        mesh=mesh,
        in_specs=(rows, rows, rows, rows, P()),
        out_specs=(rows, rows, rows, rows, P()),
        check_vma=False,
    )
```
